512 devices in a mesh: ctx: 128 (over y, x, z_lo), tp: 4 (over z_hi, core).
Axes of the slice: x: 4, y: 4, z: 16 (z_hi: 2, z_lo: 8; z = z_hi * 8 + z_lo), core: 2. Of those that a mesh axis runs over, the one named last changes fastest.
Arguments:
- hidden: bfloat16 [32768, 8192], P('ctx', 'tp'), may hold values from -6 to 6
- queries: bfloat16 [32768, 4096], P('ctx', 'tp'), may hold values from -1000 to 1000
- kv_weight: bfloat16 [8192, 1024], P('tp', 'ctx'), may hold values from -0.0625 to 0.0625
- kv_bias: bfloat16 [1024], P('tp'), may hold values from -3 to 3
- window: int32 [4], P('tp'), may hold values from 1024 to 4096, as said below
- segment_ids: int32 [32768], P('ctx'), may hold values from 0 to 15, never falling along the last dimension, each value on 1 to 4096 neighbouring positions
Outputs:
- attended: bfloat16 [32768, 4096], P('ctx', 'tp')
- kv_cache: bfloat16 [32768, 1024], P('ctx', 'tp')
The draws below stay inside these ranges and needn't reach their ends.
Inputs may be any that keep to these rules, and one draw needn't show every extreme that they name: `window`: each entry is 1024 to 4096; some key head's entry equals 4096.
All inputs are finite; a program needn't handle non-finite values.
Results may differ from the reference program's by a relative error of at most 0.012.
Values may be sent and summed in bfloat16 or wider, within the bound.
No kernel may reach another device: no remote copies, remote signals or barrier semaphores. Data moves between devices by JAX's collectives and lax.ppermute only.
A program may use at most 64 MiB of HBM per device.

```python
import math
import jax
import jax.numpy as jnp
import numpy as np
from jax import lax

D = 8192
HD = 128
KVH = 4
QPK = 8
WINDOW = 4096
TOK_DEV = 256
TOKENS = 32768
HALO = 16
N_CTX = 128


def draw_window(key, part):
    first_key, second_key = jax.random.split(jax.random.fold_in(key, 11))
    widths = jax.random.randint(first_key, (KVH,), WINDOW // 4, WINDOW + 1)
    longest = jax.random.randint(second_key, (), 0, KVH)
    return jnp.where(jnp.arange(KVH) == longest, WINDOW, widths).astype(jnp.int32)


def draw_queries(key, part):
    subkeys = jax.random.split(jax.random.fold_in(key, 12), 1)
    normals = jnp.clip(jax.random.normal(subkeys[0], (TOKENS, KVH * QPK * HD), jnp.float32), -6.0, 6.0)
    return normals.astype(jnp.bfloat16)


def levels(stream_key, extent, pieces, smallest, largest):
    gain, own = 1.0, jax.random.fold_in(stream_key, 6)
    for axis_at, parts in pieces:
        draws = jnp.exp(jax.random.uniform(jax.random.fold_in(own, axis_at), (parts,), jnp.float32, smallest / len(pieces), largest / len(pieces)))
        gain = gain * jnp.repeat(draws, extent[axis_at] // parts).reshape([-1 if axis == axis_at else 1 for axis in range(len(extent))])
    return gain


def profile(amount, total, most, lean):
    portions = [(1 << 20) // math.isqrt(grade ** lean) + 1 for grade in range(2, amount + 1)]
    rest, given = total - most - (amount - 1), [1] * (amount - 1)
    while rest > 0:
        movable = [i for i in range(amount - 1) if given[i] < most]
        pool, budget = sum([portions[i] for i in movable]), rest
        for i in movable:
            addition = min(most - given[i], max(1, budget * portions[i] // pool), rest)
            given[i] = given[i] + addition
            rest = rest - addition
    return np.array([most] + given)


def uneven_parts(rng, amount, total, bound, skew):
    if amount == 2:
        one = jax.random.randint(rng, (), max(1, total - bound), min(bound, total - 1) + 1)
        return jnp.stack([one, total - one])
    lengths = jnp.asarray(profile(amount, total, bound, skew), jnp.int32)
    couples = (amount - 1) // 2
    giver, taker = lengths[1:1 + 2 * couples:2], lengths[2:2 + 2 * couples:2]
    slack = jnp.minimum(giver - 1, bound - taker)
    passed = jax.random.randint(jax.random.fold_in(rng, 1), (couples,), 0, 1 << 20) % (slack + 1)
    lengths = lengths.at[1:1 + 2 * couples:2].set(giver - passed).at[2:2 + 2 * couples:2].set(taker + passed)
    return lengths[jax.random.permutation(jax.random.fold_in(rng, 2), amount)]


def gaussian(key, extent, spread, most, shards=(), held_as=jnp.bfloat16):
    values = spread * jax.random.normal(key, extent, jnp.float32)
    if shards:
        values = values * levels(key, extent, shards, -0.22, 0.18)
    return jnp.clip(values, -most, most).astype(held_as)


def setup_inputs(seed: int = 0) -> dict:
    key_of = jax.random.split(jax.random.key(seed), 7)
    return {
        "hidden": gaussian(key_of[0], (TOKENS, D), 1.0, 6.0, ((0, 128), (1, 4))),
        "queries": draw_queries(jax.random.fold_in(key_of[6], 71), 0),
        "kv_weight": gaussian(key_of[2], (D, KVH * 2 * HD), D ** -0.5, 0.0625, ((0, 4), (1, 128))),
        "kv_bias": gaussian(key_of[3], (KVH * 2 * HD,), 0.5, 3.0, ((0, 4),)),
        "window": draw_window(jax.random.fold_in(key_of[6], 71), 0),
        "segment_ids": jnp.searchsorted(jnp.cumsum(uneven_parts(key_of[5], max(4, TOKENS // (WINDOW // 2)), TOKENS, min(WINDOW, TOKENS // 2), 1)), jnp.arange(TOKENS), side="right").astype(jnp.int32),
    }


rope_base = 1000000.0


def rotate(values, positions):
    half = values.shape[-1] // 2
    freqs = rope_base ** (-2.0 * jnp.arange(half, dtype=jnp.float32) / values.shape[-1])
    angles = positions.astype(jnp.float32)[:, None, None] * freqs[None, None, :]
    cosine = jnp.cos(angles)
    sine = jnp.sin(angles)
    former = values[..., :half]
    latter = values[..., half:]
    return jnp.concatenate([former * cosine - latter * sine, latter * cosine + former * sine], axis=-1)


def reference(hidden, queries, kv_weight, kv_bias, window, segment_ids):
    projected = jnp.dot(hidden, kv_weight, preferred_element_type=jnp.float32) + kv_bias.astype(jnp.float32)[None, :]
    projected = projected.reshape(TOKENS, KVH, 2, HD)
    positions = jnp.arange(TOKENS, dtype=jnp.int32)
    rotated = rotate(projected[:, :, 0], positions)
    cache = jnp.stack([rotated, projected[:, :, 1]], axis=2).astype(jnp.bfloat16)
    cache = lax.optimization_barrier(cache)
    padding = HALO * TOK_DEV
    padded = jnp.concatenate([jnp.zeros((padding, KVH, 2, HD), jnp.bfloat16), cache], axis=0)
    padded_seg = jnp.concatenate([jnp.full((padding,), -1, jnp.int32), segment_ids], axis=0)
    query_all = queries.reshape(TOKENS, KVH, QPK, HD)

    def one_block(block):
        start = (block * TOK_DEV).astype(jnp.int32)
        keys_here = lax.dynamic_slice_in_dim(padded, start, padding + TOK_DEV, 0).astype(jnp.float32)
        seg_here = lax.dynamic_slice_in_dim(padded_seg, start, padding + TOK_DEV, 0)
        key_pos = start - padding + jnp.arange(padding + TOK_DEV, dtype=jnp.int32)
        query_here = lax.dynamic_slice_in_dim(query_all, start, TOK_DEV, 0).astype(jnp.float32)
        query_pos = start + jnp.arange(TOK_DEV, dtype=jnp.int32)
        query_seg = lax.dynamic_slice_in_dim(segment_ids, start, TOK_DEV, 0)
        scores = jnp.einsum("tkgd,skd->ktgs", query_here, keys_here[:, :, 0]) * HD ** -0.5
        gap = query_pos[:, None] - key_pos[None, :]
        allowed = (query_seg[:, None] == seg_here[None, :]) & (gap >= 0) & (key_pos >= 0)[None, :]
        allowed = allowed[None, :, None, :] & (gap[None, :, None, :] < window[:, None, None, None])
        scores = jnp.where(allowed, scores, -jnp.inf)
        highest = jnp.max(scores, axis=-1, keepdims=True)
        probs = jnp.exp(scores - highest)
        totals = jnp.sum(probs, axis=-1)
        rounded = lax.optimization_barrier(probs.astype(jnp.bfloat16)).astype(jnp.float32)
        mixed = jnp.einsum("ktgs,skd->tkgd", rounded, keys_here[:, :, 1])
        mixed = mixed / jnp.transpose(totals, (1, 0, 2))[..., None]
        return mixed.astype(jnp.bfloat16).reshape(TOK_DEV, KVH * QPK * HD)

    attended = lax.map(one_block, jnp.arange(N_CTX, dtype=jnp.int32)).reshape(TOKENS, KVH * QPK * HD)
    return attended, cache.reshape(TOKENS, KVH * 2 * HD)
```

```python
import jax
import jax.numpy as jnp
from jax import lax
from jax.sharding import Mesh, PartitionSpec as P

rope_base = 1000000.0
NY, NX, NZ = 4, 4, 8
ROWS = NY * NX
SEGS = 16


def gathered(part, axis, count):
    copies = jnp.broadcast_to(part[None], (count,) + part.shape)
    return lax.all_to_all(copies, axis, 0, 0, tiled=True)


def next_row(value):
    return lax.ppermute(value, ("y", "x"), [(i, i + 1) for i in range(ROWS - 1)])


def rotate(values, positions):
    half = values.shape[-1] // 2
    freqs = rope_base ** (-2.0 * jnp.arange(half, dtype=jnp.float32) / values.shape[-1])
    angles = positions.astype(jnp.float32)[:, None] * freqs[None, :]
    cosine = jnp.cos(angles)
    sine = jnp.sin(angles)
    former = values[:, :half]
    latter = values[:, half:]
    return jnp.concatenate(
        [former * cosine - latter * sine, latter * cosine + former * sine], axis=1
    )


def attend(carry, query_rows, query_pos, query_start, block, block_pos):
    running_max, running_sum, weighted = carry
    head = block.shape[1] // 2
    scores = lax.dot_general(
        query_rows, block[:, :head], (((1,), (1,)), ((), ())), preferred_element_type=jnp.float32
    )
    scores = scores * head ** (-0.5)
    allowed = (block_pos[None, :] >= query_start[:, None]) & (
        block_pos[None, :] <= query_pos[:, None]
    )
    scores = jnp.where(allowed, scores, -jnp.inf)
    newest = jnp.maximum(running_max, jnp.max(scores, axis=1))
    probs = jnp.exp(scores - newest[:, None])
    rescale = jnp.exp(running_max - newest)
    summed = running_sum * rescale + jnp.sum(probs, axis=1)
    mixed = jnp.dot(probs.astype(jnp.bfloat16), block[:, head:], preferred_element_type=jnp.float32)
    return (newest, summed, weighted * rescale[:, None] + mixed)


def body(hidden, queries, kv_weight, kv_bias, window, segment_ids):
    tok_rows = hidden.shape[0]
    feats = hidden.shape[1]
    head = kv_bias.shape[0] // 2
    z = lax.axis_index("zl")
    row = lax.axis_index("y") * NX + lax.axis_index("x")
    zh = lax.axis_index("zh")
    core = lax.axis_index("core")
    shard = row * NZ + z
    positions = shard * tok_rows + jnp.arange(tok_rows, dtype=jnp.int32)

    below = jnp.sum(
        (segment_ids[:, None] < jnp.arange(SEGS, dtype=jnp.int32)[None, :]).astype(jnp.int32), axis=0
    )
    doc_start = lax.psum(below, ("y", "x", "zl"))
    token_start = jnp.sum(
        jnp.where(
            segment_ids[:, None] == jnp.arange(SEGS, dtype=jnp.int32)[None, :], doc_start[None, :], 0
        ),
        axis=1,
    )
    token_start = jnp.maximum(token_start, positions - window[0] + 1)

    line = gathered(kv_weight.T, "zl", NZ)
    half = feats // 2
    first = line[:, :, :half]
    second = line[:, :, half:]
    first = gathered(first, "x", NX)
    second = gathered(second, "y", NY)
    first = gathered(first, "y", NY).reshape(-1, half)
    second = gathered(second, "x", NX)
    second = jnp.swapaxes(second, 0, 1).reshape(-1, half)
    last_dims = (((1,), (1,)), ((), ()))
    terms = lax.dot_general(
        hidden[:, :half], first, last_dims, preferred_element_type=jnp.float32
    ) + lax.dot_general(hidden[:, half:], second, last_dims, preferred_element_type=jnp.float32)

    width = 2 * head
    quarter = [terms[:, g * width : (g + 1) * width] for g in range(4)]
    lower = core == 0
    sent = jnp.concatenate(
        [jnp.where(lower, quarter[1], quarter[0]), jnp.where(lower, quarter[3], quarter[2])], axis=1
    )
    kept = jnp.concatenate(
        [jnp.where(lower, quarter[0], quarter[1]), jnp.where(lower, quarter[2], quarter[3])], axis=1
    )
    chip = kept + lax.ppermute(sent, "core", [(0, 1), (1, 0)])
    near = zh == 0
    far = jnp.where(near, chip[:, width:], chip[:, :width]).astype(jnp.bfloat16)
    far = lax.ppermute(far, "zh", [(0, 1), (1, 0)])
    projected = jnp.where(near, chip[:, :width], chip[:, width:]) + far.astype(jnp.float32)
    projected = projected + kv_bias.astype(jnp.float32)[None, :]
    cache = jnp.concatenate(
        [rotate(projected[:, :head], positions), projected[:, head:]], axis=1
    ).astype(jnp.bfloat16)

    older = next_row(cache)
    slots = jnp.arange(NZ, dtype=jnp.int32)
    outgoing = jnp.where((slots >= z)[:, None, None], cache[None], older[None])
    recent = lax.all_to_all(outgoing, "zl", 0, 0, tiled=True)
    earlier = next_row(jnp.concatenate([recent, older[None]], axis=0))
    recent_shard = jnp.where(slots <= z, row * NZ, (row - 1) * NZ) + slots
    offsets = jnp.arange(tok_rows, dtype=jnp.int32)

    group = queries.shape[1] // head
    query_rows = queries.reshape(tok_rows * group, head)
    query_pos = jnp.repeat(positions, group)
    query_start = jnp.repeat(token_start, group)
    row_count = tok_rows * group
    carry = (
        jnp.full((row_count,), -1e30, jnp.float32),
        jnp.zeros((row_count,), jnp.float32),
        jnp.zeros((row_count, head), jnp.float32),
    )
    for slot in range(NZ):
        block_pos = recent_shard[slot] * tok_rows + offsets
        carry = attend(carry, query_rows, query_pos, query_start, recent[slot], block_pos)
    for slot in range(NZ):
        block_pos = (recent_shard[slot] - NZ) * tok_rows + offsets
        carry = attend(carry, query_rows, query_pos, query_start, earlier[slot], block_pos)
    block_pos = (shard - 2 * NZ) * tok_rows + offsets
    carry = attend(carry, query_rows, query_pos, query_start, earlier[NZ], block_pos)
    newest, summed, weighted = carry
    attended = (weighted / summed[:, None]).reshape(tok_rows, group * head).astype(jnp.bfloat16)
    return (attended, cache)


def solution(mesh):
    fine = Mesh(mesh.devices.reshape(NY, NX, NZ, 2, 2), ("y", "x", "zl", "zh", "core"))
    ctx, tp = ("y", "x", "zl"), ("zh", "core")
    in_specs = (P(ctx, tp), P(ctx, tp), P(tp, ctx), P(tp), P(tp), P(ctx))
    out_specs = (P(ctx, tp), P(ctx, tp))
    return jax.shard_map(body, mesh=fine, in_specs=in_specs, out_specs=out_specs, check_vma=False)
```

```python
import functools

import jax
import jax.numpy as jnp
import numpy as np
from jax import lax
from jax.experimental import pallas as pl
from jax.experimental.pallas import tpu as pltpu
from jax.sharding import Mesh, PartitionSpec as P

rope_base = 1000000.0
NY, NX, NP = 4, 4, 4
ROWS = NY * NX
PAIRS = ROWS * NP
SEGS = 16
EXTRA = 128
TOK, HEAD, GROUP = 256, 128, 8
PAIR = 2 * TOK
LOG2E = 1.4426950408889634


def gathered(part, axis, count):
    copies = jnp.broadcast_to(part[None], (count,) + part.shape)
    return lax.all_to_all(copies, axis, 0, 0, tiled=True)


def next_row(value, steps):
    return lax.ppermute(value, ("y", "x"), [(i, i + steps) for i in range(ROWS - steps)])


def pairs_back(value, steps):
    moves = [(i, i + steps) for i in range(PAIRS - steps)]
    return lax.ppermute(value, ("y", "x", "zp"), moves)


def swapped(value, axis):
    return lax.ppermute(value, axis, [(0, 1), (1, 0)])


def column_order(parity):
    matrix = np.zeros((HEAD, HEAD), np.float32)
    for d in range(HEAD):
        x, z, j = d // 64, (d % 64) // 8, d % 8
        other = (z % 2) ^ parity
        matrix[d, other * 64 + x * 32 + (z // 2) * 8 + j] = 1.0
    return matrix


def flash_kernel(mine_sizes, theirs_sizes, first, last, base_ref, q_ref, start_ref, *refs):
    mine = [(ref, n) for ref, size in zip(refs, mine_sizes) for n in range(size)]
    refs = refs[len(mine_sizes) :]
    theirs = [(ref, n) for ref, size in zip(refs, theirs_sizes) for n in range(size)]
    refs = refs[len(theirs_sizes) :]
    order_ref = refs[0]
    refs = refs[1:]
    if not first:
        m_in, l_in, o_in = refs[:3]
        refs = refs[3:]
    count = len(mine)
    lanes = lax.broadcasted_iota(jnp.int32, (TOK, HEAD), 1)
    rows = lax.broadcasted_iota(jnp.int32, (TOK, HEAD), 0)
    factor = HEAD ** (-0.5) * LOG2E
    if first:
        own = pl.ds(pl.multiple_of(base_ref[count + 1], TOK), TOK)
        held = jnp.concatenate([mine[0][0][0, own, :], theirs[0][0][0, own, :]], axis=1)
        cache = jnp.dot(held, order_ref[...], preferred_element_type=jnp.float32)
        refs[3][...] = cache.astype(jnp.bfloat16)

    def keys_of(b):
        (one, n), (two, m) = mine[b], theirs[b]
        return jnp.concatenate([one[n], two[m]], axis=1)

    for h in range(GROUP):
        cols = slice(h * HEAD, (h + 1) * HEAD)
        q = q_ref[:, 2 * h * HEAD : 2 * (h + 1) * HEAD]
        tiles = []
        for b in range(count):
            s = lax.dot_general(
                q, keys_of(b), (((1,), (1,)), ((), ())), preferred_element_type=jnp.float32
            )
            for part in range(PAIR // HEAD):
                t = s[:, part * HEAD : (part + 1) * HEAD]
                key = lanes + (base_ref[b] + part * HEAD)
                ok = key >= start_ref[...]
                if first and b == 0:
                    ok = ok & (key <= rows + base_ref[count])
                tiles.append(jnp.where(ok, t, -jnp.inf))
        top = functools.reduce(jnp.maximum, tiles)
        peak = jnp.max(top, axis=1, keepdims=True)
        if not first:
            old = m_in[h][:, :1]
            peak = jnp.maximum(peak, old)
        peak = jnp.maximum(peak, -1e30)
        wide = jnp.broadcast_to(peak, (TOK, HEAD))
        probs = [jnp.exp2((t - wide) * factor) for t in tiles]
        total = jnp.sum(functools.reduce(jnp.add, probs), axis=1, keepdims=True)
        mixed = None
        per = PAIR // HEAD
        for b in range(count):
            p = jnp.concatenate(probs[per * b : per * (b + 1)], axis=1).astype(jnp.bfloat16)
            d = jnp.dot(p, keys_of(b), preferred_element_type=jnp.float32)
            mixed = d if mixed is None else mixed + d
        half = HEAD // 2
        mixed = jnp.concatenate([mixed[:, half:HEAD], mixed[:, HEAD + half :]], axis=1)
        if not first:
            scale = jnp.exp2((old - peak) * factor)
            total = total + l_in[h][:, :1] * scale
            mixed = mixed + o_in[:, cols] * scale
        if last:
            refs[1][h * TOK : (h + 1) * TOK, :] = (mixed * (1.0 / total)).astype(jnp.bfloat16)
        else:
            refs[0][h] = jnp.broadcast_to(peak, (TOK, HEAD))
            refs[1][h] = jnp.broadcast_to(total, (TOK, HEAD))
            refs[2][:, cols] = mixed
    if last:
        for h in range(GROUP):
            rows_of = slice(h * TOK, (h + 1) * TOK)
            placed = jnp.dot(refs[1][rows_of, :], order_ref[...], preferred_element_type=jnp.float32)
            refs[0][:, h * HEAD : (h + 1) * HEAD] = placed.astype(jnp.bfloat16)


def flash(queries, start, scalars, mine, theirs, order, state):
    first = state is None
    vmem = pl.BlockSpec(memory_space=pltpu.VMEM)
    operands = [queries, start, *mine, *theirs, order, *(state or ())]
    if first:
        out = [jax.ShapeDtypeStruct((GROUP, TOK, HEAD), jnp.float32)] * 2
        out.append(jax.ShapeDtypeStruct((TOK, GROUP * HEAD), jnp.float32))
        out.append(jax.ShapeDtypeStruct((TOK, 2 * HEAD), jnp.bfloat16))
    else:
        out = [jax.ShapeDtypeStruct((TOK, GROUP * HEAD), jnp.bfloat16)]
    mine_sizes = [m.shape[0] for m in mine]
    theirs_sizes = [m.shape[0] for m in theirs]
    keys = sum(mine_sizes) * PAIR
    return pl.pallas_call(
        functools.partial(flash_kernel, mine_sizes, theirs_sizes, first, not first),
        out_shape=out,
        in_specs=[pl.BlockSpec(memory_space=pltpu.SMEM)] + [vmem] * len(operands),
        out_specs=[vmem] * len(out),
        scratch_shapes=[] if first else [pltpu.VMEM((GROUP * TOK, HEAD), jnp.bfloat16)],
        compiler_params=pltpu.CompilerParams(vmem_limit_bytes=40 * 1024 * 1024),
        cost_estimate=pl.CostEstimate(
            flops=8 * GROUP * TOK * keys * HEAD,
            bytes_accessed=4 << 20,
            transcendentals=GROUP * TOK * keys,
        ),
    )(jnp.stack(scalars), *operands)


def body(hidden, queries, kv_weight, kv_bias, window, segment_ids):
    feats = hidden.shape[1]
    pz = lax.axis_index("zp")
    parity = lax.axis_index("zq")
    row = lax.axis_index("y") * NX + lax.axis_index("x")
    zh = lax.axis_index("zh")
    core = lax.axis_index("core")
    even = parity == 0
    pair = row * NP + pz
    pair_pos = pair * PAIR + jnp.arange(PAIR, dtype=jnp.int32)
    base = pair * PAIR + parity * TOK
    positions = base + jnp.arange(TOK, dtype=jnp.int32)

    partner = swapped(hidden, "zq")
    tokens = jnp.concatenate(
        [jnp.where(even, hidden, partner), jnp.where(even, partner, hidden)], axis=0
    )

    ids = jnp.arange(SEGS, dtype=jnp.int32)
    below = jnp.sum((segment_ids[:, None] < ids[None, :]).astype(jnp.float32), axis=0)
    below = jnp.pad(below.astype(jnp.bfloat16), (0, EXTRA - SEGS))

    count = kv_weight.shape[1]
    beside = jnp.broadcast_to(below[None, :], (count, EXTRA))
    line = gathered(jnp.concatenate([kv_weight.T, beside], axis=1), "zp", NP)
    whole = gathered(line, ("y", "x"), ROWS).reshape(-1, feats + EXTRA)
    terms = lax.dot_general(
        tokens, whole[:, :feats], (((1,), (1,)), ((), ())), preferred_element_type=jnp.float32
    )
    counted = jnp.sum(whole[::count, feats : feats + SEGS].astype(jnp.float32), axis=0)
    high = jnp.floor(counted / 128.0)
    digits = jnp.concatenate([high, counted - 128.0 * high]).astype(jnp.bfloat16)

    quarter = [terms[:, g * HEAD : (g + 1) * HEAD] for g in range(4)]
    lower = core == 0
    sent = jnp.concatenate(
        [jnp.where(lower, quarter[1], quarter[0]), jnp.where(lower, quarter[3], quarter[2])], axis=1
    )
    kept = jnp.concatenate(
        [jnp.where(lower, quarter[0], quarter[1]), jnp.where(lower, quarter[2], quarter[3])], axis=1
    )
    chip = kept + swapped(sent, "core")
    near = zh == 0
    far = jnp.where(near, chip[:, HEAD:], chip[:, :HEAD]).astype(jnp.bfloat16)
    far = swapped(far, "zh")
    projected = jnp.where(near, chip[:, :HEAD], chip[:, HEAD:]) + far.astype(jnp.float32)

    def of_parity(values):
        parts = values.reshape(-1, NP, 2, 8)
        return jnp.where(even, parts[:, :, 0], parts[:, :, 1]).reshape(-1)

    projected = projected + of_parity(kv_bias.astype(jnp.float32))[None, :]
    freqs = rope_base ** (-2.0 * jnp.arange(HEAD // 2, dtype=jnp.float32) / HEAD)
    angles = pair_pos.astype(jnp.float32)[:, None] * of_parity(freqs)[None, :]
    cosine = jnp.cos(angles)
    sine = jnp.sin(angles)
    former = projected[:, :32]
    latter = projected[:, 32:64]
    unit = jnp.concatenate(
        [former * cosine - latter * sine, latter * cosine + former * sine, projected[:, 64:]], axis=1
    ).astype(jnp.bfloat16)

    back = [pairs_back(unit, steps) for steps in (1, 2, 3)]
    back8 = next_row(unit, 2)
    near_mine = jnp.stack([unit] + back)
    tail = jnp.zeros((16, HEAD), jnp.bfloat16).at[0, : 2 * SEGS].set(digits)
    packed = jnp.concatenate([unit] + back + [back8, tail], axis=0)
    packed_theirs = swapped(packed, "zq")
    near_theirs = packed_theirs[: 5 * PAIR].reshape(5, PAIR, HEAD)
    far_mine = next_row(near_mine, 1)
    far_theirs = [next_row(near_theirs[:2], 1), swapped(far_mine[2:], "zq")]

    digits = packed_theirs[5 * PAIR, : 2 * SEGS].astype(jnp.float32)
    doc_start = (counted + 128.0 * digits[:SEGS] + digits[SEGS:]).astype(jnp.int32)
    token_start = jnp.sum(
        jnp.where(segment_ids[:, None] == ids[None, :], doc_start[None, :], 0), axis=1
    )
    token_start = jnp.maximum(token_start, positions - window[0] + 1)

    order = jnp.where(
        even,
        jnp.asarray(column_order(0), jnp.bfloat16),
        jnp.asarray(column_order(1), jnp.bfloat16),
    )
    gap = jnp.zeros((HEAD, HEAD // 2), jnp.bfloat16)
    spread = jnp.concatenate([order[:, : HEAD // 2], gap, order[:, HEAD // 2 :], gap], axis=1)
    wide_q = jnp.dot(
        queries.reshape(TOK * GROUP, HEAD), spread, preferred_element_type=jnp.float32
    ).astype(jnp.bfloat16)
    wide_q = wide_q.reshape(TOK, 2 * GROUP * HEAD)
    back_order = order.T

    half = HEAD // 2
    none = jnp.zeros((half, HEAD), jnp.bfloat16)
    cache_order = jnp.concatenate(
        [
            jnp.concatenate([back_order[:half], none, back_order[half:], none], axis=0),
            jnp.concatenate([none, back_order[:half], none, back_order[half:]], axis=0),
        ],
        axis=1,
    )
    start = jnp.broadcast_to(token_start[:, None], (TOK, HEAD))
    scalars = [(pair - steps) * PAIR for steps in (0, 1, 2, 3, 8)] + [base, parity * TOK]
    near_all = packed[: 5 * PAIR].reshape(5, PAIR, HEAD)
    *state, cache = flash(wide_q, start, scalars, [near_all], [near_theirs], cache_order, None)
    scalars = [(pair - steps) * PAIR for steps in (4, 5, 6, 7)]
    (attended,) = flash(wide_q, start, scalars, [far_mine], far_theirs, back_order, state)
    return (attended, cache)


def solution(mesh):
    axes = ("y", "x", "zp", "zq", "zh", "core")
    fine = Mesh(mesh.devices.reshape(NY, NX, NP, 2, 2, 2), axes)
    ctx, tp = ("y", "x", "zp", "zq"), ("zh", "core")
    in_specs = (P(ctx, tp), P(ctx, tp), P(tp, ctx), P(tp), P(tp), P(ctx))
    out_specs = (P(ctx, tp), P(ctx, tp))
    return jax.shard_map(body, mesh=fine, in_specs=in_specs, out_specs=out_specs, check_vma=False)
```
